512 devices in a mesh: cuts: 4 (over z_hi), dev: 128 (over z_lo, x, y, core).
Axes of the slice: x: 4, y: 4, z: 16 (z_hi: 4, z_lo: 4; z = z_hi * 4 + z_lo), core: 2. Of those that a mesh axis runs over, the one named last changes fastest.
Arguments:
- hidden: bfloat16 [65536, 13824], P(('cuts', 'dev')), may hold values from -6 to 6
- stream: bfloat16 [65536, 5120], P(('cuts', 'dev')), may hold values from -6 to 6
- adapter_in: bfloat16 [32, 13824], P(None, 'dev'), may hold values from -0.0546875 to 0.0546875
- adapter_out: bfloat16 [32, 5120], P(None, 'dev'), may hold values from -1 to 1
- norm_gain: float32 [1, 5120], P(None, 'dev'), may hold values from 0.5 to 1.5
- teacher: float32 [512], P(('cuts', 'dev')), may hold values from -4 to 4
Outputs:
- grad_in: float32 [32, 13824], P(None, 'dev')
- grad_out: float32 [32, 5120], P(None, 'dev')
- grad_gain: float32 [1, 5120], P(None, 'dev')
The draws below stay inside these ranges and needn't reach their ends.
All inputs are finite; a program needn't handle non-finite values.
Results may differ from the reference program's by a relative error of at most 0.024.
Values may be sent and summed in bfloat16 or wider, within the bound.
No kernel may reach another device: no remote copies, remote signals or barrier semaphores. Data moves between devices by JAX's collectives and lax.ppermute only.
A program may use at most 64 MiB of HBM per device.

```python
import jax
import jax.numpy as jnp
from jax import lax

D = 5120
FF = 13824
R = 32
QLEN = 32
PLEN = 48
GROUPS_DEV = 1
TOK_DEV = 128
GROUPS = 512
TOKENS = 65536
N_CUTS = 4
N_DEV = 128


def steps_of(stream_key, extent, cuts, least, largest):
    loudness = 1.0
    for axis_at, shards_of in cuts:
        steps = jax.random.uniform(jax.random.fold_in(jax.random.fold_in(stream_key, 6), axis_at), (shards_of,), jnp.float32, least / len(cuts), largest / len(cuts))
        loudness = loudness * jnp.repeat(jnp.exp(steps), extent[axis_at] // shards_of).reshape((-1,) + (1,) * (len(extent) - 1 - axis_at))
    return loudness


def noise(rng, dims, deviation, most, cuts=(), dtype=jnp.bfloat16):
    gain = steps_of(rng, dims, cuts, -0.22, 0.18) if cuts else 1.0
    entries = jax.random.normal(rng, dims, jnp.float32) * deviation * gain
    return jnp.minimum(jnp.maximum(entries, -most), most).astype(dtype)


def setup_inputs(seed: int = 0) -> dict:
    splits = jax.random.split(jax.random.key(seed), 7)
    return {
        "hidden": noise(splits[0], (TOKENS, FF), 1.0, 6.0, ((0, 512),)),
        "stream": noise(splits[1], (TOKENS, D), 1.0, 6.0, ((0, 512),)),
        "adapter_in": noise(splits[2], (R, FF), FF ** -0.5, 0.0546875, ((1, 128),)),
        "adapter_out": noise(splits[3], (R, D), R ** -0.5, 1.0, ((1, 128),)),
        "norm_gain": jnp.clip(1.0 + 0.1 * jax.random.normal(splits[4], (1, D), jnp.float32), 0.5, 1.5),
        "teacher": jnp.clip(jax.random.uniform(splits[5], (GROUPS,), jnp.float32, -4.0, 4.0) * steps_of(splits[5], (GROUPS,), ((0, 512),), -0.4, 0.0), -4.0, 4.0),
    }


def local_grads(hidden, stream, adapter_in, adapter_out, norm_gain, teacher):
    groups = teacher.shape[0]
    seq_tok = QLEN + 2 * PLEN
    low_rank = jnp.dot(hidden, adapter_in.T, preferred_element_type=jnp.float32).astype(jnp.bfloat16)
    summed = stream.astype(jnp.float32) + jnp.dot(low_rank, adapter_out, preferred_element_type=jnp.float32)
    inv_rms = lax.rsqrt(lax.optimization_barrier(jnp.mean(summed * summed, axis=-1, keepdims=True)) + 1e-06)
    unit = summed * inv_rms
    normed = unit * norm_gain
    blocks = normed.reshape(groups, seq_tok, D)
    query = lax.optimization_barrier(jnp.mean(blocks[:, :QLEN], axis=1))
    positive = lax.optimization_barrier(jnp.mean(blocks[:, QLEN:QLEN + PLEN], axis=1))
    negative = lax.optimization_barrier(jnp.mean(blocks[:, QLEN + PLEN:], axis=1))
    margin = lax.optimization_barrier(jnp.sum(query * (positive - negative), axis=-1))
    error = (margin - teacher)[:, None]
    d_query = error * (positive - negative) / QLEN
    d_pos = error * query / PLEN
    d_neg = -error * query / PLEN
    d_normed = jnp.concatenate([jnp.broadcast_to(d_query[:, None], (groups, QLEN, D)), jnp.broadcast_to(d_pos[:, None], (groups, PLEN, D)), jnp.broadcast_to(d_neg[:, None], (groups, PLEN, D))], axis=1).reshape(groups * seq_tok, D)
    grad_gain = lax.optimization_barrier(jnp.sum(d_normed * unit, axis=0, keepdims=True))
    d_unit = d_normed * norm_gain
    d_summed = ((d_unit - unit * lax.optimization_barrier(jnp.mean(d_unit * unit, axis=-1, keepdims=True))) * inv_rms).astype(jnp.bfloat16)
    grad_out = jnp.dot(low_rank.T, d_summed, preferred_element_type=jnp.float32)
    d_low = jnp.dot(d_summed, adapter_out.T, preferred_element_type=jnp.float32).astype(jnp.bfloat16)
    grad_in = jnp.dot(d_low.T, hidden, preferred_element_type=jnp.float32)
    return (grad_in, grad_out, grad_gain)

def reference(hidden, stream, adapter_in, adapter_out, norm_gain, teacher):
    steps_count = N_CUTS * N_DEV
    hidden_blocks = hidden.reshape(steps_count, TOK_DEV, FF)
    stream_blocks = stream.reshape(steps_count, TOK_DEV, D)
    teacher_blocks = teacher.reshape(steps_count, GROUPS_DEV)

    def accumulate(carry, items):
        part_in, part_out, part_gain = local_grads(items[0], items[1], adapter_in, adapter_out, norm_gain, items[2])
        return ((carry[0] + part_in, carry[1] + part_out, carry[2] + part_gain), None)
    start = (jnp.zeros((R, FF), jnp.float32), jnp.zeros((R, D), jnp.float32), jnp.zeros((1, D), jnp.float32))
    totals, _ = lax.scan(accumulate, start, (hidden_blocks, stream_blocks, teacher_blocks))
    return (totals[0], totals[1], totals[2])
```

```python
import jax
import jax.numpy as jnp
from jax import lax
from jax.experimental import pallas as pl
from jax.experimental.pallas import tpu as pltpu
from jax.sharding import Mesh, PartitionSpec as P

QLEN = 32
PLEN = 48
TOK = QLEN + 2 * PLEN
D = 5120
FF = 13824
R = 32
NZ, NX, NY, NC = 4, 4, 4, 2
NXY = NX * NY
WF = FF // (NZ * NXY * NC)
WD = D // (NZ * NXY * NC)
HD = WD // 2
FZ = FF // NZ
DZ = D // NZ
BLK = 40
LANE = 128
STEP = 512
DEV = ("zl", "x", "y", "c")
ALL = ("zh",) + DEV
f32 = jnp.float32
bf16 = jnp.bfloat16


def lanes(rows):
    return lax.broadcasted_iota(jnp.int32, (rows, LANE), 1)


def roll(value, shift):
    shift %= LANE
    return value if shift == 0 else pltpu.roll(value, shift, axis=1)


def block_of(a, left, tail):
    top = jnp.where(lanes(R) < WF, a, left)
    n = lanes(8)
    low = tail[3]
    for g in (2, 1, 0):
        low = jnp.where(n < HD * (g + 1), tail[g], low)
    low = jnp.where(n >= 4 * HD, tail[4], low)
    return jnp.concatenate([top, low], axis=0)


def pack_kernel(a_ref, o_ref, g_ref, out_ref, a_s, o_s, g_s):
    a_s[...] = jnp.zeros_like(a_s)
    o_s[...] = jnp.zeros_like(o_s)
    g_s[...] = jnp.zeros_like(g_s)
    a_s[:, :WF] = a_ref[...].astype(f32)
    o_s[:, :WD] = o_ref[...].astype(f32)
    g_s[:, :WD] = jnp.broadcast_to(g_ref[...], (8, WD))
    o = o_s[...]
    tail = [roll(o[8 * g : 8 * g + 8], HD * g - HD) for g in range(4)]
    tail.append(roll(g_s[...], 4 * HD))
    b = block_of(a_s[...], roll(o, WF), tail)
    two = jnp.concatenate([b, b], axis=0).astype(bf16)
    for k in range(NZ * NC // 2):
        out_ref[2 * BLK * k : 2 * BLK * (k + 1), :] = two


def window(ref, rows, base, lo, width, at):
    t, s = divmod(lo, LANE)
    tile = ref[rows, pl.ds(pl.multiple_of(base + LANE * t, LANE), LANE)]
    if s + width > LANE:
        nxt = ref[rows, pl.ds(pl.multiple_of(base + LANE * (t + 1), LANE), LANE)]
        tile = jnp.where(lanes(tile.shape[0]) >= s, tile, nxt)
    return roll(tile, at - s)


class Tiles:
    def __init__(self, rows, emit):
        self.rows, self.emit, self.tile, self.t = rows, emit, None, 0

    def add(self, piece, at, lo, width):
        t, s = divmod(lo, LANE)
        moved = roll(piece, s - at)
        if t == self.t and self.tile is not None:
            self.tile = jnp.where(lanes(self.rows) >= s, moved, self.tile)
        else:
            self.t, self.tile = t, moved
        if s + width >= LANE:
            self.emit(t, self.tile)
            self.t, self.tile = t + 1, (moved if s + width > LANE else None)


def main_kernel(
    teacher_ref, msg_ref, hidden_hbm, stream_hbm, send_ref, keep_ref,
    hidden, stream, a_in, a_out, gain, unit, rows, grad_in, grad_out, grad_gain, sems,
):
    get_hidden = pltpu.make_async_copy(hidden_hbm, hidden, sems.at[0])
    get_stream = pltpu.make_async_copy(stream_hbm, stream, sems.at[1])
    get_hidden.start()
    get_stream.start()
    core = lax.axis_index("c")

    @pl.loop(0, NZ)
    def _(z):
        def put_in(t, tile):
            a_in[:, pl.ds(pl.multiple_of(z * FZ + LANE * t, LANE), LANE)] = tile.astype(bf16)

        def put_out(t, tile):
            a_out[:, pl.ds(pl.multiple_of(z * DZ + LANE * t, LANE), LANE)] = tile.astype(bf16)

        def put_gain(t, tile):
            gain[:, pl.ds(pl.multiple_of(z * DZ + LANE * t, LANE), LANE)] = tile

        ins, outs, gains = Tiles(R, put_in), Tiles(R, put_out), Tiles(8, put_gain)
        for i in range(NXY):
            at = pl.multiple_of((i * NZ + z) * (NC * BLK), NC * BLK)
            pair = msg_ref[pl.ds(at, NC * BLK), :].astype(f32)
            for c in range(NC):
                b = pair[BLK * c : BLK * c + BLK]
                ins.add(b[:R], 0, WF * (NC * i + c), WF)
                lo = WD * (NC * i + c)
                outs.add(b[:R], WF, lo, HD)
                low = b[R:]
                outs.add(
                    jnp.concatenate([roll(low, -HD * g) for g in range(4)], axis=0),
                    0, lo + HD, HD,
                )
                gains.add(low, 4 * HD, lo, WD)

    get_hidden.wait()

    def low_step(z, acc):
        cols = pl.ds(pl.multiple_of(z * FZ, LANE), FZ)
        return acc + lax.dot_general(
            hidden[:, cols], a_in[:, cols], (((1,), (1,)), ((), ())), preferred_element_type=f32
        )

    low = lax.fori_loop(0, NZ, low_step, jnp.zeros((TOK, R), f32)).astype(bf16)
    get_stream.wait()

    def sum_step(k, acc):
        cols = pl.ds(pl.multiple_of(k * STEP, LANE), STEP)
        s = stream[:, cols].astype(f32) + jnp.dot(low, a_out[:, cols], preferred_element_type=f32)
        unit[:, cols] = s
        for t in range(STEP // LANE):
            x = s[:, LANE * t : LANE * (t + 1)]
            acc = acc + x * x
        return acc

    squares = lax.fori_loop(0, D // STEP, sum_step, jnp.zeros((TOK, LANE), f32))
    inv = lax.rsqrt(jnp.sum(squares, axis=1, keepdims=True) / D + 1e-06)

    def unit_step(k, carry):
        margin, acc = carry
        cols = pl.ds(pl.multiple_of(k * STEP, LANE), STEP)
        u = unit[:, cols] * inv
        unit[:, cols] = u
        g = gain[:1, cols]
        uq = jnp.sum(u[:QLEN], axis=0, keepdims=True) / QLEN
        up = jnp.sum(u[QLEN : QLEN + PLEN], axis=0, keepdims=True) / PLEN
        un = jnp.sum(u[QLEN + PLEN :], axis=0, keepdims=True) / PLEN
        q = g * uq
        pn = g * (up - un)
        margin = margin + q * pn
        wq = pn * g / QLEN
        wp = q * g / PLEN
        rows[0:1, cols] = wq
        rows[1:2, cols] = wp
        rows[2:3, cols] = uq * pn
        prod = jnp.concatenate(
            [u[:QLEN] * wq, u[QLEN : QLEN + PLEN] * wp, u[QLEN + PLEN :] * -wp], axis=0
        )
        for t in range(STEP // LANE):
            acc = acc + prod[:, LANE * t : LANE * (t + 1)]
        return margin, acc

    margin, acc = lax.fori_loop(
        0, D // STEP, unit_step, (jnp.zeros((1, STEP), f32), jnp.zeros((TOK, LANE), f32))
    )
    err = jnp.sum(margin, axis=1, keepdims=True) - teacher_ref[0]
    mean = jnp.sum(acc, axis=1, keepdims=True) / D
    scale = inv * err

    def grad_step(k, acc):
        cols = pl.ds(pl.multiple_of(k * STEP, LANE), STEP)
        um = unit[:, cols] * mean
        wq = rows[0:1, cols]
        wp = rows[1:2, cols]
        d = jnp.concatenate(
            [wq - um[:QLEN], wp - um[QLEN : QLEN + PLEN], -wp - um[QLEN + PLEN :]], axis=0
        )
        d = (d * scale).astype(bf16)
        grad_out[:, cols] = lax.dot_general(
            low, d, (((0,), (0,)), ((), ())), preferred_element_type=f32
        )
        grad_gain[:, cols] = jnp.broadcast_to(2.0 * err * rows[2:3, cols], (8, STEP))
        return acc + lax.dot_general(
            d, a_out[:, cols], (((1,), (1,)), ((), ())), preferred_element_type=f32
        )

    d_low = lax.fori_loop(0, D // STEP, grad_step, jnp.zeros((TOK, R), f32)).astype(bf16)

    @pl.loop(0, NZ)
    def _(z):
        cols = pl.ds(pl.multiple_of(z * FZ, LANE), FZ)
        grad_in[:, cols] = lax.dot_general(
            d_low, hidden[:, cols], (((0,), (0,)), ((), ())), preferred_element_type=f32
        )

    @pl.loop(0, NZ // 2)
    def _(h):
        every = slice(None)
        for i in range(NXY):
            blocks = []
            for c in range(NC):
                pair = []
                for z2 in range(2):
                    z = 2 * h + z2
                    lo = WD * (NC * i + c)
                    a = window(grad_in, every, z * FZ, WF * (NC * i + c), WF, 0)
                    left = window(grad_out, every, z * DZ, lo, HD, WF)
                    tail = [
                        window(grad_out, slice(8 * g, 8 * g + 8), z * DZ, lo + HD, HD, HD * g)
                        for g in range(4)
                    ]
                    tail.append(window(grad_gain, every, z * DZ, lo, WD, 4 * HD))
                    pair.append(block_of(a, left, tail))
                blocks.append(jnp.concatenate(pair, axis=0))
            at = pl.ds(pl.multiple_of(NZ * BLK * i + 2 * BLK * h, 2 * BLK), 2 * BLK)
            first = core == 0
            send_ref[at, :] = jnp.where(first, blocks[1], blocks[0]).astype(bf16)
            keep_ref[at, :] = jnp.where(first, blocks[0], blocks[1]).astype(bf16)


def sum_xy_kernel(in_ref, out_ref):
    n = NZ * BLK
    acc = in_ref[:n].astype(f32)
    for k in range(1, NXY):
        acc = acc + in_ref[n * k : n * (k + 1)].astype(f32)
    out_ref[...] = acc.astype(bf16)


def sum_four(in_ref):
    x = in_ref[...].astype(f32)
    return (x[:BLK] + x[BLK : 2 * BLK]) + (x[2 * BLK : 3 * BLK] + x[3 * BLK :])


def sum_z_kernel(in_ref, out_ref):
    acc = sum_four(in_ref)
    out_ref[...] = jnp.concatenate([acc] * 4, axis=0).astype(bf16)


def final_kernel(in_ref, a_ref, o_ref, g_ref):
    b = sum_four(in_ref)
    low = b[R:]
    a_ref[...] = b[:R, :WF]
    left = roll(b[:R], -WF)
    right = jnp.concatenate([roll(low, HD - HD * g) for g in range(4)], axis=0)
    o_ref[...] = jnp.where(lanes(R) < HD, left, right)[:, :WD]
    g_ref[...] = roll(low, -4 * HD)[:1, :WD]


VMEM = pl.BlockSpec(memory_space=pltpu.VMEM)
ANY = pl.BlockSpec(memory_space=pl.ANY)
SMEM = pl.BlockSpec(memory_space=pltpu.SMEM)


def call(kernel, shapes, *args, specs=None, scratch=(), limit=None):
    return pl.pallas_call(
        kernel,
        out_shape=shapes,
        in_specs=specs or [VMEM] * len(args),
        out_specs=jax.tree.map(lambda _: VMEM, shapes),
        scratch_shapes=list(scratch),
        compiler_params=pltpu.CompilerParams(vmem_limit_bytes=limit) if limit else None,
    )(*args)


def shape(rows, cols, dtype=bf16):
    return jax.ShapeDtypeStruct((rows, cols), dtype)


def body(hidden, stream, adapter_in, adapter_out, norm_gain, teacher):
    mine = call(
        pack_kernel, shape(NZ * NC * BLK, LANE), adapter_in, adapter_out, norm_gain,
        scratch=[pltpu.VMEM((R, LANE), f32), pltpu.VMEM((R, LANE), f32), pltpu.VMEM((8, LANE), f32)],
    )
    column = lax.all_to_all(mine, ("zl", "c"), 0, 0, tiled=True)
    copies = jnp.broadcast_to(column[None], (NXY, NZ * NC * BLK, LANE))
    msg = lax.all_to_all(copies, ("x", "y"), 0, 0, tiled=True)
    msg = msg.reshape(NXY * NZ * NC * BLK, LANE)
    half = NXY * NZ * BLK
    send, keep = call(
        main_kernel, (shape(half, LANE), shape(half, LANE)), teacher, msg, hidden, stream,
        specs=[SMEM, VMEM, ANY, ANY],
        scratch=[
            pltpu.VMEM((TOK, FF), bf16),
            pltpu.VMEM((TOK, D), bf16),
            pltpu.VMEM((R, FF), bf16),
            pltpu.VMEM((R, D), bf16),
            pltpu.VMEM((8, D), f32),
            pltpu.VMEM((TOK, D), f32),
            pltpu.VMEM((8, D), f32),
            pltpu.VMEM((R, FF), f32),
            pltpu.VMEM((R, D), f32),
            pltpu.VMEM((8, D), f32),
            pltpu.SemaphoreType.DMA((2,)),
        ],
        limit=40 * 2**20,
    )
    other = lax.ppermute(send, "c", [(0, 1), (1, 0)])
    pairs = (keep.astype(f32) + other.astype(f32)).astype(bf16)
    parts = lax.all_to_all(pairs, ("x", "y"), 0, 0, tiled=True)
    part = call(sum_xy_kernel, shape(NZ * BLK, LANE), parts)
    part = lax.all_to_all(part, "zl", 0, 0, tiled=True)
    part = call(sum_z_kernel, shape(4 * BLK, LANE), part)
    part = lax.all_to_all(part, "zh", 0, 0, tiled=True)
    return call(final_kernel, (shape(R, WF, f32), shape(R, WD, f32), shape(1, WD, f32)), part)


def solution(mesh):
    fine = Mesh(mesh.devices.reshape(4, NZ, NX, NY, NC), ALL)
    return jax.shard_map(
        body,
        mesh=fine,
        in_specs=(P(ALL, None), P(ALL, None), P(None, DEV), P(None, DEV), P(None, DEV), P(ALL)),
        out_specs=(P(None, DEV), P(None, DEV), P(None, DEV)),
        check_vma=False,
    )
```

```python
import jax
import jax.numpy as jnp
from jax import lax
from jax.experimental import pallas as pl
from jax.experimental.pallas import tpu as pltpu
from jax.sharding import Mesh, PartitionSpec as P

QLEN = 32
PLEN = 48
TOK = QLEN + 2 * PLEN
D = 5120
FF = 13824
R = 32
NH = 4
NZ, NX, NY, NC = 4, 4, 4, 2
NXY = NX * NY
NK = NZ * NXY
WF = FF // (NK * NC)
WD = D // (NK * NC)
NG = WD // 8
FZ = FF // NZ
DZ = D // NZ
BLK = 48
LANE = 128
CH = NG * LANE
NCH = D // CH
DEV = ("zl", "x", "y", "c")
ALL = ("zh",) + DEV
SWAP = [(0, 1), (1, 0)]
f32 = jnp.float32
bf16 = jnp.bfloat16


def lanes(rows):
    return lax.broadcasted_iota(jnp.int32, (rows, LANE), 1)


def roll(value, shift):
    shift %= LANE
    return value if shift == 0 else pltpu.roll(value, shift, axis=1)


def dot(a, b):
    return jnp.dot(a, b, preferred_element_type=f32)


def dot_t(a, b):
    return lax.dot_general(a, b, (((1,), (1,)), ((), ())), preferred_element_type=f32)


def eye(n):
    i = lax.broadcasted_iota(jnp.int32, (n, n), 0)
    j = lax.broadcasted_iota(jnp.int32, (n, n), 1)
    return (i == j).astype(f32).astype(bf16)


def pack_kernel(a_ref, o_ref, g_ref, out_ref, a_s, o_s):
    a_s[...] = jnp.zeros_like(a_s)
    o_s[...] = jnp.zeros_like(o_s)
    a_s[:, :WF] = a_ref[...].astype(f32)
    o_s[:R, :WD] = o_ref[...].astype(f32)
    o_s[R : R + 1, :WD] = g_ref[...]
    t = o_s[...].T
    n = lanes(8)
    one = [t[8 * g : 8 * g + 8] for g in range(NG)]
    low = one[0]
    for g in range(1, 4):
        low = jnp.where(n < R * g, low, roll(one[g], R * g))
    high = one[4]
    for g in range(NG):
        high = jnp.where(n == R + g, roll(one[g], g), high)
    block = jnp.concatenate([a_s[...], low, high], axis=0).astype(bf16)
    for k in range(NZ):
        out_ref[k] = block


def stream_kernel(stream_ref, stream_out, perm):
    first = lax.axis_index("c") == 0
    n = lanes(1)
    row = lax.broadcasted_iota(jnp.int32, (DZ, LANE), 0)
    for own in range(NC):
        for g in range(NG):
            c = jnp.where(first, own, 1 - own)
            at = (n // 8) * (NC * WD) + n % 8 + c * WD + 8 * g
            t = own * NG + g
            perm[:, LANE * t : LANE * (t + 1)] = (row == at).astype(f32).astype(bf16)
    for z in range(NZ):
        cols = slice(DZ * z, DZ * (z + 1))
        stream_out[:, cols] = dot(stream_ref[:, cols], perm[...]).astype(bf16)


def hidden_kernel(hidden_ref, hidden_out):
    first = lax.axis_index("c") == 0
    inside = lanes(TOK) < WF
    for i in range(NXY):
        both = []
        for c in range(NC):
            t, s = divmod(WF * (NC * i + c), LANE)
            tile = hidden_ref[:, LANE * t : LANE * (t + 1)].astype(f32)
            if s + WF > LANE:
                nxt = hidden_ref[:, LANE * (t + 1) : LANE * (t + 2)].astype(f32)
                tile = jnp.where(lanes(TOK) >= s, tile, nxt)
            both.append(jnp.where(inside, roll(tile, -s), 0.0))
        cols = slice(LANE * i, LANE * (i + 1))
        hidden_out[0, 0, :, cols] = jnp.where(first, both[0], both[1]).astype(bf16)
        hidden_out[1, 0, :, cols] = jnp.where(first, both[1], both[0]).astype(bf16)


def main_kernel(
    teacher_ref, mine_ref, other_ref, hidden_hbm, stream_ref, keep_ref, send_ref,
    hidden, a_out, gain, unit, rows, grad_out, grad_gain, sems,
):
    blocks = (mine_ref, other_ref)
    copies = {}
    for own in range(NC):
        for z in range(NZ):
            copies[own, z] = pltpu.make_async_copy(
                hidden_hbm.at[own, z], hidden.at[own, z], sems.at[own * NZ + z]
            )
            copies[own, z].start()
    chunks = [(z, own) for z in range(NZ) for own in range(NC)]
    one = eye(LANE)
    k8 = 8

    for n, (z, own) in enumerate(chunks):
        x = blocks[own][:, z, R:, :].astype(f32)
        low = dot_t(one, x[:, :8].reshape(LANE, LANE).astype(bf16))
        high = dot_t(one, x[:, 8:].reshape(LANE, LANE).astype(bf16))
        for g in range(NG):
            cols = slice(CH * n + LANE * g, CH * n + LANE * (g + 1))
            a_out[:, cols] = (low[R * g : R * g + R] if g < 4 else high[:R]).astype(bf16)
            gain[:, cols] = jnp.broadcast_to(high[R + g : R + g + 1], (8, LANE))

    acc = jnp.zeros((TOK, R), f32)
    for own in range(NC):
        for k in range(0, NK, k8):
            z, i = divmod(k, NXY)
            if i == 0:
                copies[own, z].wait()
            a = jnp.concatenate([blocks[own][i + m, z, :R, :] for m in range(k8)], axis=1)
            acc = acc + dot_t(hidden[own, z, :, LANE * i : LANE * (i + k8)], a)
    low = acc.astype(bf16)
    low_t = dot_t(eye(R), low).astype(bf16)

    squares = jnp.zeros((TOK, LANE), f32)
    for n in range(NCH):
        cols = slice(CH * n, CH * (n + 1))
        s = stream_ref[:, cols].astype(f32) + dot(low, a_out[:, cols])
        unit[:, cols] = s
        for g in range(NG):
            x = s[:, LANE * g : LANE * (g + 1)]
            squares = squares + x * x
    inv = lax.rsqrt(jnp.sum(squares, axis=1, keepdims=True) / D + 1e-06)

    margin = jnp.zeros((1, CH), f32)
    acc = jnp.zeros((TOK, LANE), f32)
    for n in range(NCH):
        cols = slice(CH * n, CH * (n + 1))
        u = unit[:, cols] * inv
        unit[:, cols] = u
        gn = gain[:1, cols]
        uq = jnp.sum(u[:QLEN], axis=0, keepdims=True) / QLEN
        up = jnp.sum(u[QLEN : QLEN + PLEN], axis=0, keepdims=True) / PLEN
        un = jnp.sum(u[QLEN + PLEN :], axis=0, keepdims=True) / PLEN
        q = gn * uq
        pn = gn * (up - un)
        margin = margin + q * pn
        wq = pn * gn / QLEN
        wp = q * gn / PLEN
        rows[0:1, cols] = wq
        rows[1:2, cols] = wp
        rows[2:3, cols] = uq * pn
        prod = jnp.concatenate(
            [u[:QLEN] * wq, u[QLEN : QLEN + PLEN] * wp, u[QLEN + PLEN :] * -wp], axis=0
        )
        for g in range(NG):
            acc = acc + prod[:, LANE * g : LANE * (g + 1)]
    err = jnp.sum(margin, axis=1, keepdims=True) - teacher_ref[0]
    mean = jnp.sum(acc, axis=1, keepdims=True) / D
    scale = inv * err

    grad_gain[...] = jnp.zeros_like(grad_gain)
    acc = jnp.zeros((R, TOK), f32)
    for n in range(NCH):
        cols = slice(CH * n, CH * (n + 1))
        um = unit[:, cols] * mean
        wq = rows[0:1, cols]
        wp = rows[1:2, cols]
        d = jnp.concatenate(
            [wq - um[:QLEN], wp - um[QLEN : QLEN + PLEN], -wp - um[QLEN + PLEN :]], axis=0
        )
        d = (d * scale).astype(bf16)
        acc = acc + dot_t(a_out[:, cols], d)
        grad_out[:, cols] = dot(low_t, d).astype(bf16)
        gg = 2.0 * err * rows[2:3, cols]
        for g in range(NG):
            grad_gain[g : g + 1, LANE * n : LANE * (n + 1)] = gg[:, LANE * g : LANE * (g + 1)]
    d_low = acc.astype(bf16)

    outs = (keep_ref, send_ref)
    for own in (1, 0):
        for k in range(0, NK, k8):
            z, i = divmod(k, NXY)
            x = dot(d_low, hidden[own, z, :, LANE * i : LANE * (i + k8)]).astype(bf16)
            for m in range(k8):
                outs[own][i + m, z, :R, :] = x[:, LANE * m : LANE * (m + 1)]

    for n, (z, own) in enumerate(chunks):
        x = [grad_out[:, CH * n + LANE * g : CH * n + LANE * (g + 1)] for g in range(NG)]
        low = dot_t(one, jnp.concatenate(x[:4], axis=0))
        gg = grad_gain[:, LANE * n : LANE * (n + 1)].astype(bf16)
        zero = jnp.zeros((LANE - R - 16, LANE), bf16)
        high = dot_t(one, jnp.concatenate([x[4], gg, zero], axis=0))
        y = jnp.concatenate([low.reshape(NXY, 8, LANE), high.reshape(NXY, 8, LANE)], axis=1)
        outs[own][:, z, R:, :] = y.astype(bf16)


def final_kernel(in_ref, a_ref, o_ref, g_ref):
    b = jnp.sum(in_ref[...].astype(f32), axis=0)
    a_ref[...] = b[:R, :WF]
    low = b[R : R + 8]
    high = b[R + 8 :]
    n = lanes(8)
    parts = []
    for g in range(NG):
        part = roll(low, -R * g) if g < 4 else high
        parts.append(jnp.where(n == R, roll(high, -g), part))
    parts.append(jnp.zeros((LANE - 8 * NG, LANE), f32))
    t = jnp.concatenate(parts, axis=0).T
    o_ref[...] = t[:R, :WD]
    g_ref[...] = t[R : R + 1, :WD]


VMEM = pl.BlockSpec(memory_space=pltpu.VMEM)
SMEM = pl.BlockSpec(memory_space=pltpu.SMEM)


def call(kernel, shapes, *args, in_specs=None, out_specs=None, limit=None, **more):
    return pl.pallas_call(
        kernel,
        out_shape=shapes,
        in_specs=in_specs or [VMEM] * len(args),
        out_specs=out_specs or jax.tree.map(lambda _: VMEM, shapes),
        compiler_params=pltpu.CompilerParams(vmem_limit_bytes=limit) if limit else None,
        **more,
    )(*args)


def shape(*dims, dtype=bf16):
    return jax.ShapeDtypeStruct(dims, dtype)


def place_stream(stream):
    return call(
        stream_kernel, shape(TOK, D), stream,
        scratch_shapes=[pltpu.VMEM((DZ, DZ), bf16)],
        cost_estimate=pl.CostEstimate(flops=2 * TOK * D * DZ, bytes_accessed=4 * TOK * D, transcendentals=0),
        limit=16 * 2**20,
    )


def place_hidden(hidden):
    return call(
        hidden_kernel, shape(NC, NZ, TOK, NXY * LANE), hidden,
        grid=(NZ,),
        in_specs=[pl.BlockSpec((TOK, FZ), lambda z: (0, z))],
        out_specs=pl.BlockSpec((NC, 1, TOK, NXY * LANE), lambda z: (0, z, 0, 0)),
        cost_estimate=pl.CostEstimate(flops=TOK * FF * 8, bytes_accessed=6 * TOK * FF, transcendentals=0),
        limit=60 * 2**20,
    )


def local(teacher, mine, other, hidden, stream):
    return call(
        main_kernel, (shape(NXY, NZ, BLK, LANE), shape(NXY, NZ, BLK, LANE)), teacher, mine, other, hidden, stream,
        in_specs=[SMEM, VMEM, VMEM, pl.BlockSpec(memory_space=pl.ANY), VMEM],
        scratch_shapes=[
            pltpu.VMEM((NC, NZ, TOK, NXY * LANE), bf16),
            pltpu.VMEM((R, D), bf16),
            pltpu.VMEM((8, D), f32),
            pltpu.VMEM((TOK, D), f32),
            pltpu.VMEM((8, D), f32),
            pltpu.VMEM((R, D), bf16),
            pltpu.VMEM((16, NCH * LANE), f32),
            pltpu.SemaphoreType.DMA((NC * NZ,)),
        ],
        limit=46 * 2**20,
    )


def body(hidden, stream, adapter_in, adapter_out, norm_gain, teacher):
    mine = call(
        pack_kernel, shape(NZ, BLK, LANE), adapter_in, adapter_out, norm_gain,
        scratch_shapes=[pltpu.VMEM((R, LANE), f32), pltpu.VMEM((LANE, LANE), f32)],
    )
    column = lax.all_to_all(mine, "zl", 0, 0, tiled=True)
    column = column.reshape(1, NZ * BLK, LANE)
    copies = jnp.broadcast_to(column, (NXY, NZ * BLK, LANE))
    mine = lax.all_to_all(copies, ("x", "y"), 0, 0, tiled=True)
    mine, hidden, stream = lax.optimization_barrier(
        (mine, place_hidden(hidden), place_stream(stream))
    )
    mine = mine.reshape(NXY, NZ, BLK, LANE)
    other = lax.ppermute(mine, "c", SWAP)
    keep, send = local(teacher, mine, other, hidden, stream)
    other = lax.ppermute(send, "c", SWAP)
    pairs = (keep.astype(f32) + other.astype(f32)).astype(bf16)
    pairs = pairs.reshape(NXY, NZ * BLK, LANE)
    parts = lax.all_to_all(pairs, ("x", "y"), 0, 0, tiled=True)
    part = jnp.sum(parts.astype(f32), axis=0).astype(bf16)
    part = part.reshape(1, NZ, BLK, LANE)
    parts = jnp.broadcast_to(part, (NH, NZ, BLK, LANE)).reshape(NH * NZ, BLK, LANE)
    parts = lax.all_to_all(parts, ("zh", "zl"), 0, 0, tiled=True)
    shapes = (shape(R, WF, dtype=f32), shape(R, WD, dtype=f32), shape(1, WD, dtype=f32))
    return call(final_kernel, shapes, parts)


def solution(mesh):
    fine = Mesh(mesh.devices.reshape(NH, NZ, NX, NY, NC), ALL)
    return jax.shard_map(
        body,
        mesh=fine,
        in_specs=(P(ALL, None), P(ALL, None), P(None, DEV), P(None, DEV), P(None, DEV), P(ALL)),
        out_specs=(P(None, DEV), P(None, DEV), P(None, DEV)),
        check_vma=False,
    )
```

```python
import jax
import jax.numpy as jnp
from jax import lax
from jax.experimental import pallas as pl
from jax.experimental.pallas import tpu as pltpu
from jax.sharding import Mesh, PartitionSpec as P

QLEN = 32
PLEN = 48
TOK = QLEN + 2 * PLEN
D = 5120
FF = 13824
R = 32
NH = 4
NZ, NX, NY, NC = 4, 4, 4, 2
NXY = NX * NY
NK = NZ * NXY
WF = FF // (NK * NC)
WD = D // (NK * NC)
NG = WD // 8
FZ = FF // NZ
DZ = D // NZ
BLK = 40
LANE = 128
LAST = 108
GAIN = 116
TOP = NZ * R
CH = NG * LANE
NCH = D // CH
DEV = ("zl", "x", "y", "c")
ALL = ("zh",) + DEV
SWAP = [(0, 1), (1, 0)]
f32 = jnp.float32
bf16 = jnp.bfloat16


def lanes(rows):
    return lax.broadcasted_iota(jnp.int32, (rows, LANE), 1)


def roll(value, shift):
    shift %= LANE
    return value if shift == 0 else pltpu.roll(value, shift, axis=1)


def dot(a, b):
    return jnp.dot(a, b, preferred_element_type=f32)


def dot_t(a, b):
    return lax.dot_general(a, b, (((1,), (1,)), ((), ())), preferred_element_type=f32)


def eye(n):
    i = lax.broadcasted_iota(jnp.int32, (n, n), 0)
    j = lax.broadcasted_iota(jnp.int32, (n, n), 1)
    return (i == j).astype(f32).astype(bf16)


def pack_kernel(a_ref, o_ref, g_ref, out_ref, a_s, o_s):
    a_s[...] = jnp.zeros_like(a_s)
    o_s[...] = jnp.zeros_like(o_s)
    a_s[:, :WF] = a_ref[...].astype(f32)
    o_s[:R, :WD] = o_ref[...].astype(f32)
    o_s[R : R + 1, :WD] = g_ref[...]
    o = o_s[...]
    t = o.T
    one = [t[8 * g : 8 * g + 8] for g in range(NG)]
    n = lanes(R)
    top = jnp.where(n < LAST, a_s[...], jnp.where(n < GAIN, roll(o[:R], LAST - R), 0.0))
    n = lanes(8)
    low, gains = one[0], top[:8]
    for g in range(1, 4):
        low = jnp.where(n < R * g, low, roll(one[g], R * g))
    for g in range(NG):
        gains = jnp.where(n == GAIN + g, roll(one[g], GAIN + g - R), gains)
    block = jnp.concatenate([gains, top[8:], low], axis=0).astype(bf16)
    for k in range(NZ):
        out_ref[k] = block


def stream_kernel(stream_ref, stream_out, perm):
    first = lax.axis_index("c") == 0
    n = lanes(1)
    row = lax.broadcasted_iota(jnp.int32, (DZ, LANE), 0)
    for own in range(NC):
        for g in range(NG):
            c = jnp.where(first, own, 1 - own)
            at = (n // 8) * (NC * WD) + n % 8 + c * WD + 8 * g
            t = own * NG + g
            perm[:, LANE * t : LANE * (t + 1)] = (row == at).astype(f32).astype(bf16)
    for z in range(NZ):
        cols = slice(DZ * z, DZ * (z + 1))
        stream_out[:, cols] = dot(stream_ref[:, cols], perm[...]).astype(bf16)


def hidden_kernel(hidden_ref, hidden_out):
    core = lax.axis_index("c")
    inside = lanes(TOK) < WF
    now, tile = -1, None
    for n in range(NXY * NC):
        t, s = divmod(WF * n, LANE)
        if t != now:
            now, tile = t, hidden_ref[:, LANE * t : LANE * (t + 1)].astype(f32)
        x = tile
        if s + WF > LANE:
            now, tile = t + 1, hidden_ref[:, LANE * (t + 1) : LANE * (t + 2)].astype(f32)
            x = jnp.where(lanes(TOK) >= s, x, tile)
        x = jnp.where(inside, roll(x, -s), 0.0).astype(bf16)
        own = core if n % NC == 0 else 1 - core
        hidden_out[own, 0, :, LANE * (n // NC) : LANE * (n // NC + 1)] = x


def main_kernel(
    teacher_ref, mine_ref, other_ref, hidden_hbm, stream_ref, keep_ref, send_ref,
    hidden, a_out, gain, unit, rows, grad_out, grad_gain, sems,
):
    blocks = (mine_ref, other_ref)
    one = eye(LANE)
    k8 = 8
    n = NXY * LANE
    spread = lax.broadcasted_iota(jnp.int32, (LANE, n), 0)
    spread = spread // 8 * LANE + spread % 8 + LAST
    spread = (spread == lax.broadcasted_iota(jnp.int32, (LANE, n), 1)).astype(f32).astype(bf16)
    copies = {}
    for own in range(NC):
        for z in range(NZ):
            copies[own, z] = pltpu.make_async_copy(
                hidden_hbm.at[own, z], hidden.at[own, z], sems.at[own * NZ + z]
            )
            copies[own, z].start()
    one = eye(LANE)
    k8 = 8

    for own in range(NC):
        top = [
            jnp.concatenate([blocks[own][i, R * z : R * (z + 1), :] for i in range(NXY)], axis=1)
            for z in range(NZ)
        ]
        last = dot_t(jnp.concatenate(top, axis=0), spread)
        low = blocks[own][:, TOP:, :].astype(f32)
        for z in range(NZ):
            n = CH * (NC * z + own)
            x = low[:, 8 * z : 8 * z + 8].reshape(LANE, LANE).astype(bf16)
            x = dot_t(one, x)
            y = blocks[own][:, R * z : R * z + 16, :].astype(f32)
            y = dot_t(one[LANE - 16 :], y[:, :8].reshape(LANE, LANE).astype(bf16))
            for g in range(NG):
                cols = slice(n + LANE * g, n + LANE * (g + 1))
                part = x[R * g : R * g + R] if g < 4 else last[R * z : R * z + R]
                a_out[:, cols] = part.astype(bf16)
                row = GAIN - LANE + 16 + g
                gain[:, cols] = jnp.broadcast_to(y[row : row + 1], (8, LANE))

    acc = jnp.zeros((TOK, R), f32)
    for own in range(NC):
        for k in range(0, NK, k8):
            z, i = divmod(k, NXY)
            if i == 0:
                copies[own, z].wait()
            a = [blocks[own][i + m, R * z : R * (z + 1), :] for m in range(k8)]
            a = jnp.concatenate(a, axis=1)
            acc = acc + dot_t(hidden[own, z, :, LANE * i : LANE * (i + k8)], a)
    low = acc.astype(bf16)
    low_t = dot_t(eye(R), low).astype(bf16)

    squares = jnp.zeros((TOK, LANE), f32)
    for n in range(NCH):
        cols = slice(CH * n, CH * (n + 1))
        s = stream_ref[:, cols].astype(f32) + dot(low, a_out[:, cols])
        unit[:, cols] = s
        for g in range(NG):
            x = s[:, LANE * g : LANE * (g + 1)]
            squares = squares + x * x
    inv = lax.rsqrt(jnp.sum(squares, axis=1, keepdims=True) / D + 1e-06)

    margin = jnp.zeros((1, CH), f32)
    acc = jnp.zeros((TOK, LANE), f32)
    for n in range(NCH):
        cols = slice(CH * n, CH * (n + 1))
        u = unit[:, cols] * inv
        unit[:, cols] = u
        gn = gain[:1, cols]
        uq = jnp.sum(u[:QLEN], axis=0, keepdims=True) / QLEN
        up = jnp.sum(u[QLEN : QLEN + PLEN], axis=0, keepdims=True) / PLEN
        un = jnp.sum(u[QLEN + PLEN :], axis=0, keepdims=True) / PLEN
        q = gn * uq
        pn = gn * (up - un)
        margin = margin + q * pn
        wq = pn * gn / QLEN
        wp = q * gn / PLEN
        rows[0:1, cols] = wq
        rows[1:2, cols] = wp
        rows[2:3, cols] = uq * pn
        prod = jnp.concatenate(
            [u[:QLEN] * wq, u[QLEN : QLEN + PLEN] * wp, u[QLEN + PLEN :] * -wp], axis=0
        )
        for g in range(NG):
            acc = acc + prod[:, LANE * g : LANE * (g + 1)]
    err = jnp.sum(margin, axis=1, keepdims=True) - teacher_ref[0]
    mean = jnp.sum(acc, axis=1, keepdims=True) / D
    scale = inv * err

    grad_gain[...] = jnp.zeros_like(grad_gain)
    acc = jnp.zeros((R, TOK), f32)
    for n in range(NCH):
        cols = slice(CH * n, CH * (n + 1))
        um = unit[:, cols] * mean
        wq = rows[0:1, cols]
        wp = rows[1:2, cols]
        d = jnp.concatenate(
            [wq - um[:QLEN], wp - um[QLEN : QLEN + PLEN], -wp - um[QLEN + PLEN :]], axis=0
        )
        d = (d * scale).astype(bf16)
        acc = acc + dot_t(a_out[:, cols], d)
        grad_out[:, cols] = dot(low_t, d).astype(bf16)
        gg = 2.0 * err * rows[2:3, cols]
        for g in range(NG):
            row = GAIN - LANE + 16 + g
            grad_gain[row : row + 1, LANE * n : LANE * (n + 1)] = gg[:, LANE * g : LANE * (g + 1)]
    d_low = acc.astype(bf16)

    outs = (keep_ref, send_ref)
    for own in (1, 0):
        low = []
        last = [CH * (NC * z + own) + LANE * (NG - 1) for z in range(NZ)]
        last = jnp.concatenate([grad_out[:, n : n + LANE] for n in last], axis=0)
        last = dot(last, spread)
        for z in range(NZ):
            n = NC * z + own
            x = [grad_out[:, CH * n + LANE * g : CH * n + LANE * (g + 1)] for g in range(4)]
            y = dot_t(one, jnp.concatenate(x, axis=0))
            low.append(y.reshape(NXY, 8, LANE))
            gg = grad_gain[:, LANE * n : LANE * (n + 1)].astype(bf16)
            gg = dot_t(one, jnp.concatenate([jnp.zeros((LANE - 16, LANE), bf16), gg], axis=0))
            for i in range(0, NXY, k8):
                cols = slice(LANE * i, LANE * (i + k8))
                top = dot(d_low, hidden[own, z, :, cols]) + last[R * z : R * (z + 1), cols]
                for m in range(k8):
                    t = top[:, LANE * m : LANE * (m + 1)]
                    t = jnp.concatenate([t[:8] + gg[8 * (i + m) : 8 * (i + m) + 8], t[8:]], axis=0)
                    outs[own][i + m, R * z : R * (z + 1), :] = t.astype(bf16)
        outs[own][:, TOP:, :] = jnp.concatenate(low, axis=1).astype(bf16)


def final_kernel(in_ref, a_ref, o_ref, g_ref):
    b = in_ref[...]
    a_ref[...] = b[:R, :WF]
    low = b[R:]
    n = lanes(8)
    parts = []
    for g in range(NG):
        part = roll(low, -R * g) if g < 4 else low
        parts.append(jnp.where(n == R, roll(b[:8], R - GAIN - g), part))
    parts.append(jnp.zeros((LANE - 8 * NG, LANE), f32))
    t = jnp.concatenate(parts, axis=0).T
    o_ref[...] = jnp.where(lanes(R) < R, t[:R], roll(b[:R], R - LAST))[:, :WD]
    g_ref[...] = t[R : R + 1, :WD]


VMEM = pl.BlockSpec(memory_space=pltpu.VMEM)
SMEM = pl.BlockSpec(memory_space=pltpu.SMEM)


def call(kernel, shapes, *args, in_specs=None, out_specs=None, limit=None, **more):
    return pl.pallas_call(
        kernel,
        out_shape=shapes,
        in_specs=in_specs or [VMEM] * len(args),
        out_specs=out_specs or jax.tree.map(lambda _: VMEM, shapes),
        compiler_params=pltpu.CompilerParams(vmem_limit_bytes=limit) if limit else None,
        **more,
    )(*args)


def shape(*dims, dtype=bf16):
    return jax.ShapeDtypeStruct(dims, dtype)


def place_stream(stream):
    return call(
        stream_kernel, shape(TOK, D), stream,
        scratch_shapes=[pltpu.VMEM((DZ, DZ), bf16)],
        cost_estimate=pl.CostEstimate(flops=2 * TOK * D * DZ, bytes_accessed=4 * TOK * D, transcendentals=0),
        limit=16 * 2**20,
    )


def place_hidden(hidden):
    return call(
        hidden_kernel, shape(NC, NZ, TOK, NXY * LANE), hidden,
        grid=(NZ,),
        in_specs=[pl.BlockSpec((TOK, FZ), lambda z: (0, z))],
        out_specs=pl.BlockSpec((NC, 1, TOK, NXY * LANE), lambda z: (0, z, 0, 0)),
        cost_estimate=pl.CostEstimate(flops=TOK * FF * 8, bytes_accessed=6 * TOK * FF, transcendentals=0),
        limit=60 * 2**20,
    )


def local(teacher, mine, other, hidden, stream):
    return call(
        main_kernel, (shape(NXY, NZ * BLK, LANE), shape(NXY, NZ * BLK, LANE)), teacher, mine, other, hidden, stream,
        in_specs=[SMEM, VMEM, VMEM, pl.BlockSpec(memory_space=pl.ANY), VMEM],
        scratch_shapes=[
            pltpu.VMEM((NC, NZ, TOK, NXY * LANE), bf16),
            pltpu.VMEM((R, D), bf16),
            pltpu.VMEM((8, D), f32),
            pltpu.VMEM((TOK, D), f32),
            pltpu.VMEM((8, D), f32),
            pltpu.VMEM((R, D), bf16),
            pltpu.VMEM((16, NCH * LANE), f32),
            pltpu.SemaphoreType.DMA((NC * NZ,)),
        ],
        limit=49 * 2**20,
    )


def body(hidden, stream, adapter_in, adapter_out, norm_gain, teacher):
    mine = call(
        pack_kernel, shape(NZ, BLK, LANE), adapter_in, adapter_out, norm_gain,
        scratch_shapes=[pltpu.VMEM((R, LANE), f32), pltpu.VMEM((LANE, LANE), f32)],
    )
    column = lax.all_to_all(mine, "zl", 0, 0, tiled=True)
    column, stream = lax.optimization_barrier((column, place_stream(stream)))
    column = jnp.concatenate(
        [column[:, :R].reshape(1, TOP, LANE), column[:, R:].reshape(1, 8 * NZ, LANE)], axis=1
    )
    copies = jnp.broadcast_to(column, (NXY, NZ * BLK, LANE))
    mine = lax.all_to_all(copies, ("x", "y"), 0, 0, tiled=True)
    mine, hidden = lax.optimization_barrier((mine, place_hidden(hidden)))
    other = lax.ppermute(mine, "c", SWAP)
    keep, send = local(teacher, mine, other, hidden, stream)
    other = lax.ppermute(send, "c", SWAP)
    pairs = (keep.astype(f32) + other.astype(f32)).astype(bf16)
    parts = lax.all_to_all(pairs, ("x", "y"), 0, 0, tiled=True)
    part = jnp.sum(parts.astype(f32), axis=0).astype(bf16)
    part = jnp.concatenate(
        [part[:TOP].reshape(1, NZ, R, LANE), part[TOP:].reshape(1, NZ, 8, LANE)], axis=2
    )
    parts = jnp.broadcast_to(part, (NH, NZ, BLK, LANE)).reshape(NH * NZ, BLK, LANE)
    parts = lax.all_to_all(parts, ("zh", "zl"), 0, 0, tiled=True)
    shapes = (shape(R, WF, dtype=f32), shape(R, WD, dtype=f32), shape(1, WD, dtype=f32))
    return call(final_kernel, shapes, jnp.sum(parts.astype(f32), axis=0))


def solution(mesh):
    fine = Mesh(mesh.devices.reshape(NH, NZ, NX, NY, NC), ALL)
    return jax.shard_map(
        body,
        mesh=fine,
        in_specs=(P(ALL, None), P(ALL, None), P(None, DEV), P(None, DEV), P(None, DEV), P(ALL)),
        out_specs=(P(None, DEV), P(None, DEV), P(None, DEV)),
        check_vma=False,
    )
```

```python
import jax
import jax.numpy as jnp
from jax import lax
from jax.experimental import pallas as pl
from jax.experimental.pallas import tpu as pltpu
from jax.sharding import Mesh, PartitionSpec as P

QLEN = 32
PLEN = 48
TOK = QLEN + 2 * PLEN
D = 5120
FF = 13824
R = 32
NH = 4
NZ, NX, NY, NC = 4, 4, 4, 2
NXY = NX * NY
NK = NZ * NXY
WF = FF // (NK * NC)
WD = D // (NK * NC)
NG = WD // 8
FZ = FF // NZ
DZ = D // NZ
BLK = 40
LANE = 128
LAST = 108
GAIN = 116
TOP = NZ * R
CH = NG * LANE
NCH = D // CH
DEV = ("zl", "x", "y", "c")
ALL = ("zh",) + DEV
SWAP = [(0, 1), (1, 0)]
f32 = jnp.float32
bf16 = jnp.bfloat16


def lanes(rows):
    return lax.broadcasted_iota(jnp.int32, (rows, LANE), 1)


def roll(value, shift):
    shift %= LANE
    return value if shift == 0 else pltpu.roll(value, shift, axis=1)


def dot(a, b):
    return jnp.dot(a, b, preferred_element_type=f32)


def dot_t(a, b):
    return lax.dot_general(a, b, (((1,), (1,)), ((), ())), preferred_element_type=f32)


def eye(n):
    i = lax.broadcasted_iota(jnp.int32, (n, n), 0)
    j = lax.broadcasted_iota(jnp.int32, (n, n), 1)
    return (i == j).astype(f32).astype(bf16)


def pack_kernel(a_ref, o_ref, g_ref, out_ref, a_s, o_s):
    a_s[...] = jnp.zeros_like(a_s)
    o_s[...] = jnp.zeros_like(o_s)
    a_s[:, :WF] = a_ref[...].astype(f32)
    o_s[:R, :WD] = o_ref[...].astype(f32)
    o_s[R : R + 1, :WD] = g_ref[...]
    o = o_s[...]
    t = o.T
    one = [t[8 * g : 8 * g + 8] for g in range(NG)]
    n = lanes(R)
    top = jnp.where(n < LAST, a_s[...], jnp.where(n < GAIN, roll(o[:R], LAST - R), 0.0))
    n = lanes(8)
    low, gains = one[0], top[:8]
    for g in range(1, 4):
        low = jnp.where(n < R * g, low, roll(one[g], R * g))
    for g in range(NG):
        gains = jnp.where(n == GAIN + g, roll(one[g], GAIN + g - R), gains)
    block = jnp.concatenate([gains, top[8:], low], axis=0).astype(bf16)
    for k in range(NZ):
        out_ref[k] = block


def stream_kernel(stream_ref, stream_out, perm):
    first = lax.axis_index("c") == 0
    n = lanes(1)
    row = lax.broadcasted_iota(jnp.int32, (DZ, LANE), 0)
    for own in range(NC):
        for g in range(NG):
            c = jnp.where(first, own, 1 - own)
            at = (n // 8) * (NC * WD) + n % 8 + c * WD + 8 * g
            t = own * NG + g
            perm[:, LANE * t : LANE * (t + 1)] = (row == at).astype(f32).astype(bf16)
    x = [stream_ref[:, DZ * z : DZ * (z + 1)] for z in range(NZ)]
    x = dot(jnp.concatenate(x, axis=0), perm[...]).astype(bf16)
    for z in range(NZ):
        stream_out[:, DZ * z : DZ * (z + 1)] = x[TOK * z : TOK * (z + 1)]


def hidden_kernel(hidden_ref, hidden_out):
    core = lax.axis_index("c")
    inside = lanes(TOK) < WF
    now, tile = -1, None
    for n in range(NXY * NC):
        t, s = divmod(WF * n, LANE)
        if t != now:
            now, tile = t, hidden_ref[:, LANE * t : LANE * (t + 1)].astype(f32)
        x = tile
        if s + WF > LANE:
            now, tile = t + 1, hidden_ref[:, LANE * (t + 1) : LANE * (t + 2)].astype(f32)
            x = jnp.where(lanes(TOK) >= s, x, tile)
        x = jnp.where(inside, roll(x, -s), 0.0).astype(bf16)
        own = core if n % NC == 0 else 1 - core
        hidden_out[own, 0, :, LANE * (n // NC) : LANE * (n // NC + 1)] = x


def main_kernel(
    teacher_ref, mine_ref, other_ref, hidden_hbm, stream_ref, keep_ref, send_ref,
    hidden, a_out, gain, summed, rows, grad_out, grad_gain, sems,
):
    blocks = (mine_ref, other_ref)
    one = eye(LANE)
    k8 = 8
    n = NXY * LANE
    spread = lax.broadcasted_iota(jnp.int32, (LANE, n), 0)
    spread = spread // 8 * LANE + spread % 8 + LAST
    spread = (spread == lax.broadcasted_iota(jnp.int32, (LANE, n), 1)).astype(f32).astype(bf16)
    copies = {}
    for own in range(NC):
        for z in range(NZ):
            copies[own, z] = pltpu.make_async_copy(
                hidden_hbm.at[own, z], hidden.at[own, z], sems.at[own * NZ + z]
            )
            copies[own, z].start()
    one = eye(LANE)
    k8 = 8

    for own in range(NC):
        top = [
            jnp.concatenate([blocks[own][i, R * z : R * (z + 1), :] for i in range(NXY)], axis=1)
            for z in range(NZ)
        ]
        last = dot_t(jnp.concatenate(top, axis=0), spread)
        low = blocks[own][:, TOP:, :].astype(f32)
        for z in range(NZ):
            n = CH * (NC * z + own)
            x = low[:, 8 * z : 8 * z + 8].reshape(LANE, LANE).astype(bf16)
            x = dot_t(one, x)
            y = blocks[own][:, R * z : R * z + 16, :].astype(f32)
            y = dot_t(one[LANE - 16 :], y[:, :8].reshape(LANE, LANE).astype(bf16))
            for g in range(NG):
                cols = slice(n + LANE * g, n + LANE * (g + 1))
                part = x[R * g : R * g + R] if g < 4 else last[R * z : R * z + R]
                a_out[:, cols] = part.astype(bf16)
                row = GAIN - LANE + 16 + g
                gain[:, cols] = jnp.broadcast_to(y[row : row + 1], (8, LANE))

    acc = jnp.zeros((TOK, R), f32)
    for own in range(NC):
        for k in range(0, NK, k8):
            z, i = divmod(k, NXY)
            if i == 0:
                copies[own, z].wait()
            a = [blocks[own][i + m, R * z : R * (z + 1), :] for m in range(k8)]
            a = jnp.concatenate(a, axis=1)
            acc = acc + dot_t(hidden[own, z, :, LANE * i : LANE * (i + k8)], a)
    low = acc.astype(bf16)
    low_t = dot_t(eye(R), low).astype(bf16)

    squares = jnp.zeros((TOK, LANE), f32)
    for n in range(NCH):
        cols = slice(CH * n, CH * (n + 1))
        s = stream_ref[:, cols].astype(f32) + dot(low, a_out[:, cols])
        summed[:, cols] = s
        for g in range(NG):
            x = s[:, LANE * g : LANE * (g + 1)]
            squares = squares + x * x
    inv = lax.rsqrt(jnp.sum(squares, axis=1, keepdims=True) / D + 1e-06)

    margin = jnp.zeros((1, CH), f32)
    acc = jnp.zeros((TOK, LANE), f32)
    for n in range(NCH):
        cols = slice(CH * n, CH * (n + 1))
        u = summed[:, cols] * inv
        gn = gain[:1, cols]
        uq = jnp.sum(u[:QLEN], axis=0, keepdims=True) / QLEN
        up = jnp.sum(u[QLEN : QLEN + PLEN], axis=0, keepdims=True) / PLEN
        un = jnp.sum(u[QLEN + PLEN :], axis=0, keepdims=True) / PLEN
        q = gn * uq
        pn = gn * (up - un)
        margin = margin + q * pn
        wq = pn * gn / QLEN
        wp = q * gn / PLEN
        rows[0:1, cols] = wq
        rows[1:2, cols] = wp
        rows[2:3, cols] = uq * pn
        prod = jnp.concatenate(
            [u[:QLEN] * wq, u[QLEN : QLEN + PLEN] * wp, u[QLEN + PLEN :] * -wp], axis=0
        )
        for g in range(NG):
            acc = acc + prod[:, LANE * g : LANE * (g + 1)]
    err = jnp.sum(margin, axis=1, keepdims=True) - teacher_ref[0]
    mean = inv * (jnp.sum(acc, axis=1, keepdims=True) / D)
    scale = inv * err

    grad_gain[...] = jnp.zeros_like(grad_gain)
    acc = jnp.zeros((TOK, R), f32)
    for n in range(NCH):
        cols = slice(CH * n, CH * (n + 1))
        um = summed[:, cols] * mean
        wq = rows[0:1, cols]
        wp = rows[1:2, cols]
        d = jnp.concatenate(
            [wq - um[:QLEN], wp - um[QLEN : QLEN + PLEN], -wp - um[QLEN + PLEN :]], axis=0
        )
        d = (d * scale).astype(bf16)
        acc = acc + dot_t(d, a_out[:, cols])
        grad_out[:, cols] = dot(low_t, d).astype(bf16)
        gg = 2.0 * err * rows[2:3, cols]
        for g in range(NG):
            row = GAIN - LANE + 16 + g
            grad_gain[row : row + 1, LANE * n : LANE * (n + 1)] = gg[:, LANE * g : LANE * (g + 1)]
    d_low = dot_t(eye(R), acc.astype(bf16)).astype(bf16)

    outs = (keep_ref, send_ref)
    for own in (1, 0):
        low = []
        last = [CH * (NC * z + own) + LANE * (NG - 1) for z in range(NZ)]
        last = jnp.concatenate([grad_out[:, n : n + LANE] for n in last], axis=0)
        last = dot(last, spread)
        for z in range(NZ):
            n = NC * z + own
            x = [grad_out[:, CH * n + LANE * g : CH * n + LANE * (g + 1)] for g in range(4)]
            y = dot_t(one, jnp.concatenate(x, axis=0))
            low.append(y.reshape(NXY, 8, LANE))
            gg = grad_gain[:, LANE * n : LANE * (n + 1)].astype(bf16)
            gg = dot_t(one, jnp.concatenate([jnp.zeros((LANE - 16, LANE), bf16), gg], axis=0))
            for i in range(0, NXY, k8):
                cols = slice(LANE * i, LANE * (i + k8))
                top = dot(d_low, hidden[own, z, :, cols]) + last[R * z : R * (z + 1), cols]
                for m in range(k8):
                    t = top[:, LANE * m : LANE * (m + 1)]
                    t = jnp.concatenate([t[:8] + gg[8 * (i + m) : 8 * (i + m) + 8], t[8:]], axis=0)
                    outs[own][i + m, R * z : R * (z + 1), :] = t.astype(bf16)
        outs[own][:, TOP:, :] = jnp.concatenate(low, axis=1).astype(bf16)


def final_kernel(in_ref, a_ref, o_ref, g_ref):
    b = jnp.sum(in_ref[...].astype(f32), axis=0)
    a_ref[...] = b[:R, :WF]
    low = b[R:]
    n = lanes(8)
    parts = []
    for g in range(NG):
        part = roll(low, -R * g) if g < 4 else low
        parts.append(jnp.where(n == R, roll(b[:8], R - GAIN - g), part))
    parts.append(jnp.zeros((LANE - 8 * NG, LANE), f32))
    t = jnp.concatenate(parts, axis=0).T
    o_ref[...] = jnp.where(lanes(R) < R, t[:R], roll(b[:R], R - LAST))[:, :WD]
    g_ref[...] = t[R : R + 1, :WD]


VMEM = pl.BlockSpec(memory_space=pltpu.VMEM)
SMEM = pl.BlockSpec(memory_space=pltpu.SMEM)


def call(kernel, shapes, *args, in_specs=None, out_specs=None, limit=None, **more):
    return pl.pallas_call(
        kernel,
        out_shape=shapes,
        in_specs=in_specs or [VMEM] * len(args),
        out_specs=out_specs or jax.tree.map(lambda _: VMEM, shapes),
        compiler_params=pltpu.CompilerParams(vmem_limit_bytes=limit) if limit else None,
        **more,
    )(*args)


def shape(*dims, dtype=bf16):
    return jax.ShapeDtypeStruct(dims, dtype)


def place_stream(stream):
    return call(
        stream_kernel, shape(TOK, D), stream,
        scratch_shapes=[pltpu.VMEM((DZ, DZ), bf16)],
        cost_estimate=pl.CostEstimate(flops=2 * TOK * D * DZ, bytes_accessed=4 * TOK * D, transcendentals=0),
        limit=16 * 2**20,
    )


def place_hidden(hidden):
    return call(
        hidden_kernel, shape(NC, NZ, TOK, NXY * LANE), hidden,
        grid=(NZ,),
        in_specs=[pl.BlockSpec((TOK, FZ), lambda z: (0, z))],
        out_specs=pl.BlockSpec((NC, 1, TOK, NXY * LANE), lambda z: (0, z, 0, 0)),
        cost_estimate=pl.CostEstimate(flops=TOK * FF * 8, bytes_accessed=6 * TOK * FF, transcendentals=0),
        limit=60 * 2**20,
    )


def local(teacher, mine, other, hidden, stream):
    return call(
        main_kernel, (shape(NXY, NZ * BLK, LANE), shape(NXY, NZ * BLK, LANE)), teacher, mine, other, hidden, stream,
        in_specs=[SMEM, VMEM, VMEM, pl.BlockSpec(memory_space=pl.ANY), VMEM],
        scratch_shapes=[
            pltpu.VMEM((NC, NZ, TOK, NXY * LANE), bf16),
            pltpu.VMEM((R, D), bf16),
            pltpu.VMEM((8, D), f32),
            pltpu.VMEM((TOK, D), f32),
            pltpu.VMEM((8, D), f32),
            pltpu.VMEM((R, D), bf16),
            pltpu.VMEM((16, NCH * LANE), f32),
            pltpu.SemaphoreType.DMA((NC * NZ,)),
        ],
        limit=49 * 2**20,
    )


def body(hidden, stream, adapter_in, adapter_out, norm_gain, teacher):
    mine = call(
        pack_kernel, shape(NZ, BLK, LANE), adapter_in, adapter_out, norm_gain,
        scratch_shapes=[pltpu.VMEM((R, LANE), f32), pltpu.VMEM((LANE, LANE), f32)],
    )
    column = lax.all_to_all(mine, "zl", 0, 0, tiled=True)
    column = jnp.concatenate(
        [column[:, :R].reshape(1, TOP, LANE), column[:, R:].reshape(1, 8 * NZ, LANE)], axis=1
    )
    copies = jnp.broadcast_to(column, (NXY, NZ * BLK, LANE))
    mine = lax.all_to_all(copies, ("x", "y"), 0, 0, tiled=True)
    mine, hidden, stream = lax.optimization_barrier(
        (mine, place_hidden(hidden), place_stream(stream))
    )
    other = lax.ppermute(mine, "c", SWAP)
    keep, send = local(teacher, mine, other, hidden, stream)
    other = lax.ppermute(send, "c", SWAP)
    pairs = (keep.astype(f32) + other.astype(f32)).astype(bf16)
    parts = lax.all_to_all(pairs, ("x", "y"), 0, 0, tiled=True)
    part = jnp.sum(parts.astype(f32), axis=0).astype(bf16)
    part = jnp.concatenate(
        [part[:TOP].reshape(1, NZ, R, LANE), part[TOP:].reshape(1, NZ, 8, LANE)], axis=2
    )
    parts = jnp.broadcast_to(part, (NH, NZ, BLK, LANE)).reshape(NH * NZ, BLK, LANE)
    parts = lax.all_to_all(parts, ("zh", "zl"), 0, 0, tiled=True)
    shapes = (shape(R, WF, dtype=f32), shape(R, WD, dtype=f32), shape(1, WD, dtype=f32))
    return call(final_kernel, shapes, parts)


def solution(mesh):
    fine = Mesh(mesh.devices.reshape(NH, NZ, NX, NY, NC), ALL)
    return jax.shard_map(
        body,
        mesh=fine,
        in_specs=(P(ALL, None), P(ALL, None), P(None, DEV), P(None, DEV), P(None, DEV), P(ALL)),
        out_specs=(P(None, DEV), P(None, DEV), P(None, DEV)),
        check_vma=False,
    )
```

```python
import jax
import jax.numpy as jnp
from jax import lax
from jax.experimental import pallas as pl
from jax.experimental.pallas import tpu as pltpu
from jax.sharding import Mesh, PartitionSpec as P

QLEN = 32
PLEN = 48
TOK = QLEN + 2 * PLEN
D = 5120
FF = 13824
R = 32
NH = 4
NZ, NX, NY, NC = 4, 4, 4, 2
NXY = NX * NY
NK = NZ * NXY
WF = FF // (NK * NC)
WD = D // (NK * NC)
NG = WD // 8
FZ = FF // NZ
DZ = D // NZ
BLK = 40
LANE = 128
LAST = 108
GAIN = 116
TOP = NZ * R
CH = NG * LANE
NCH = D // CH
DEV = ("zl", "x", "y", "c")
ALL = ("zh",) + DEV
SWAP = [(0, 1), (1, 0)]
f32 = jnp.float32
bf16 = jnp.bfloat16


def lanes(rows):
    return lax.broadcasted_iota(jnp.int32, (rows, LANE), 1)


def roll(value, shift):
    shift %= LANE
    return value if shift == 0 else pltpu.roll(value, shift, axis=1)


def dot(a, b):
    return jnp.dot(a, b, preferred_element_type=f32)


def dot_t(a, b):
    return lax.dot_general(a, b, (((1,), (1,)), ((), ())), preferred_element_type=f32)


def eye(n):
    i = lax.broadcasted_iota(jnp.int32, (n, n), 0)
    j = lax.broadcasted_iota(jnp.int32, (n, n), 1)
    return (i == j).astype(f32).astype(bf16)


def pack_kernel(a_ref, o_ref, g_ref, out_ref, a_s, o_s):
    a_s[...] = jnp.zeros_like(a_s)
    o_s[...] = jnp.zeros_like(o_s)
    a_s[:, :WF] = a_ref[...].astype(f32)
    o_s[:R, :WD] = o_ref[...].astype(f32)
    o_s[R : R + 1, :WD] = g_ref[...]
    o = o_s[...]
    t = o.T
    one = [t[8 * g : 8 * g + 8] for g in range(NG)]
    n = lanes(R)
    top = jnp.where(n < LAST, a_s[...], jnp.where(n < GAIN, roll(o[:R], LAST - R), 0.0))
    n = lanes(8)
    low, gains = one[0], top[:8]
    for g in range(1, 4):
        low = jnp.where(n < R * g, low, roll(one[g], R * g))
    for g in range(NG):
        gains = jnp.where(n == GAIN + g, roll(one[g], GAIN + g - R), gains)
    block = jnp.concatenate([gains, top[8:], low], axis=0).astype(bf16)
    for k in range(NZ):
        out_ref[k] = block


def stream_kernel(stream_ref, stream_out, perm):
    first = lax.axis_index("c") == 0
    n = lanes(1)
    row = lax.broadcasted_iota(jnp.int32, (DZ, LANE), 0)
    for own in range(NC):
        for g in range(NG):
            c = jnp.where(first, own, 1 - own)
            at = (n // 8) * (NC * WD) + n % 8 + c * WD + 8 * g
            t = own * NG + g
            perm[:, LANE * t : LANE * (t + 1)] = (row == at).astype(f32).astype(bf16)
    x = [stream_ref[:, DZ * z : DZ * (z + 1)] for z in range(NZ)]
    x = dot(jnp.concatenate(x, axis=0), perm[...]).astype(bf16)
    for z in range(NZ):
        stream_out[:, DZ * z : DZ * (z + 1)] = x[TOK * z : TOK * (z + 1)]


def hidden_kernel(hidden_ref, hidden_out):
    core = lax.axis_index("c")
    inside = lanes(TOK) < WF
    now, tile = -1, None
    for n in range(NXY * NC):
        t, s = divmod(WF * n, LANE)
        if t != now:
            now, tile = t, hidden_ref[:, LANE * t : LANE * (t + 1)].astype(f32)
        x = tile
        if s + WF > LANE:
            now, tile = t + 1, hidden_ref[:, LANE * (t + 1) : LANE * (t + 2)].astype(f32)
            x = jnp.where(lanes(TOK) >= s, x, tile)
        x = jnp.where(inside, roll(x, -s), 0.0).astype(bf16)
        own = core if n % NC == 0 else 1 - core
        hidden_out[own, 0, :, LANE * (n // NC) : LANE * (n // NC + 1)] = x


def main_kernel(
    teacher_ref, mine_ref, other_ref, hidden_hbm, stream_ref, keep_ref, send_ref,
    hidden, a_out, gain, summed, rows, grad_out, grad_gain, d_all, sems,
):
    blocks = (mine_ref, other_ref)
    one = eye(LANE)
    k8 = 8
    at = lax.broadcasted_iota(jnp.int32, (LANE, LANE), 0)
    at = (at >> 3) * LANE + (at & 7) + LAST - lanes(LANE)
    spread = [(at == LANE * i).astype(f32).astype(bf16) for i in range(NXY)]
    spread = jnp.concatenate(spread, axis=1)
    copies = {}
    for own in range(NC):
        for z in range(NZ):
            copies[own, z] = pltpu.make_async_copy(
                hidden_hbm.at[own, z], hidden.at[own, z], sems.at[own * NZ + z]
            )
            copies[own, z].start()
    one = eye(LANE)
    k8 = 8

    for own in range(NC):
        top = [
            jnp.concatenate([blocks[own][i, R * z : R * (z + 1), :] for i in range(NXY)], axis=1)
            for z in range(NZ)
        ]
        last = dot_t(jnp.concatenate(top, axis=0), spread)
        low = blocks[own][:, TOP:, :].astype(f32)
        for z in range(NZ):
            n = CH * (NC * z + own)
            x = low[:, 8 * z : 8 * z + 8].reshape(LANE, LANE).astype(bf16)
            x = dot_t(one, x)
            y = blocks[own][:, R * z : R * z + 16, :].astype(f32)
            y = dot_t(one[LANE - 16 :], y[:, :8].reshape(LANE, LANE).astype(bf16))
            for g in range(NG):
                cols = slice(n + LANE * g, n + LANE * (g + 1))
                part = x[R * g : R * g + R] if g < 4 else last[R * z : R * z + R]
                a_out[:, cols] = part.astype(bf16)
                row = GAIN - LANE + 16 + g
                gain[:, cols] = jnp.broadcast_to(y[row : row + 1], (8, LANE))

    acc = jnp.zeros((TOK, R), f32)
    for own in range(NC):
        for k in range(0, NK, k8):
            z, i = divmod(k, NXY)
            if i == 0:
                copies[own, z].wait()
            a = [blocks[own][i + m, R * z : R * (z + 1), :] for m in range(k8)]
            a = jnp.concatenate(a, axis=1)
            acc = acc + dot_t(hidden[own, z, :, LANE * i : LANE * (i + k8)], a)
    low = acc.astype(bf16)
    low_t = dot_t(eye(R), low).astype(bf16)

    squares = jnp.zeros((TOK, LANE), f32)
    for n in range(NCH):
        cols = slice(CH * n, CH * (n + 1))
        s = stream_ref[:, cols].astype(f32) + dot(low, a_out[:, cols])
        summed[:, cols] = s
        for g in range(NG):
            x = s[:, LANE * g : LANE * (g + 1)]
            squares = squares + x * x
    inv = lax.rsqrt(jnp.sum(squares, axis=1, keepdims=True) / D + 1e-06)

    margin = jnp.zeros((1, CH), f32)
    acc = jnp.zeros((TOK, LANE), f32)
    for n in range(NCH):
        cols = slice(CH * n, CH * (n + 1))
        u = summed[:, cols] * inv
        gn = gain[:1, cols]
        uq = jnp.sum(u[:QLEN], axis=0, keepdims=True) / QLEN
        up = jnp.sum(u[QLEN : QLEN + PLEN], axis=0, keepdims=True) / PLEN
        un = jnp.sum(u[QLEN + PLEN :], axis=0, keepdims=True) / PLEN
        q = gn * uq
        pn = gn * (up - un)
        margin = margin + q * pn
        wq = pn * gn / QLEN
        wp = q * gn / PLEN
        rows[0:1, cols] = wq
        rows[1:2, cols] = wp
        rows[2:3, cols] = uq * pn
        prod = jnp.concatenate(
            [u[:QLEN] * wq, u[QLEN : QLEN + PLEN] * wp, u[QLEN + PLEN :] * -wp], axis=0
        )
        for g in range(NG):
            acc = acc + prod[:, LANE * g : LANE * (g + 1)]
    err = jnp.sum(margin, axis=1, keepdims=True) - teacher_ref[0]
    mean = inv * (jnp.sum(acc, axis=1, keepdims=True) / D)
    scale = inv * err

    grad_gain[...] = jnp.zeros_like(grad_gain)
    for n in range(NCH):
        cols = slice(CH * n, CH * (n + 1))
        um = summed[:, cols] * mean
        wq = rows[0:1, cols]
        wp = rows[1:2, cols]
        d = jnp.concatenate(
            [wq - um[:QLEN], wp - um[QLEN : QLEN + PLEN], -wp - um[QLEN + PLEN :]], axis=0
        )
        d = (d * scale).astype(bf16)
        d_all[:, cols] = d
        grad_out[:, cols] = dot(low_t, d).astype(bf16)
        gg = 2.0 * err * rows[2:3, cols]
        for g in range(NG):
            row = GAIN - LANE + 16 + g
            grad_gain[row : row + 1, LANE * n : LANE * (n + 1)] = gg[:, LANE * g : LANE * (g + 1)]
    d_low = dot_t(eye(R), dot_t(d_all[...], a_out[...]).astype(bf16)).astype(bf16)

    outs = (keep_ref, send_ref)
    for own in (1, 0):
        low = []
        last = [CH * (NC * z + own) + LANE * (NG - 1) for z in range(NZ)]
        last = jnp.concatenate([grad_out[:, n : n + LANE] for n in last], axis=0)
        last = dot(last, spread)
        for z in range(NZ):
            n = NC * z + own
            x = [grad_out[:, CH * n + LANE * g : CH * n + LANE * (g + 1)] for g in range(4)]
            y = dot_t(one, jnp.concatenate(x, axis=0))
            low.append(y.reshape(NXY, 8, LANE))
            gg = grad_gain[:, LANE * n : LANE * (n + 1)].astype(bf16)
            gg = dot_t(one, jnp.concatenate([jnp.zeros((LANE - 16, LANE), bf16), gg], axis=0))
            for i in range(0, NXY, k8):
                cols = slice(LANE * i, LANE * (i + k8))
                top = dot(d_low, hidden[own, z, :, cols]) + last[R * z : R * (z + 1), cols]
                for m in range(k8):
                    t = top[:, LANE * m : LANE * (m + 1)]
                    t = jnp.concatenate([t[:8] + gg[8 * (i + m) : 8 * (i + m) + 8], t[8:]], axis=0)
                    outs[own][i + m, R * z : R * (z + 1), :] = t.astype(bf16)
        outs[own][:, TOP:, :] = jnp.concatenate(low, axis=1).astype(bf16)


def final_kernel(in_ref, a_ref, o_ref, g_ref):
    b = jnp.sum(in_ref[...].astype(f32), axis=0)
    a_ref[...] = b[:R, :WF]
    low = b[R:]
    n = lanes(8)
    parts = []
    for g in range(NG):
        part = roll(low, -R * g) if g < 4 else low
        parts.append(jnp.where(n == R, roll(b[:8], R - GAIN - g), part))
    parts.append(jnp.zeros((LANE - 8 * NG, LANE), f32))
    t = jnp.concatenate(parts, axis=0).T
    o_ref[...] = jnp.where(lanes(R) < R, t[:R], roll(b[:R], R - LAST))[:, :WD]
    g_ref[...] = t[R : R + 1, :WD]


VMEM = pl.BlockSpec(memory_space=pltpu.VMEM)
SMEM = pl.BlockSpec(memory_space=pltpu.SMEM)


def call(kernel, shapes, *args, in_specs=None, out_specs=None, limit=None, **more):
    return pl.pallas_call(
        kernel,
        out_shape=shapes,
        in_specs=in_specs or [VMEM] * len(args),
        out_specs=out_specs or jax.tree.map(lambda _: VMEM, shapes),
        compiler_params=pltpu.CompilerParams(vmem_limit_bytes=limit) if limit else None,
        **more,
    )(*args)


def shape(*dims, dtype=bf16):
    return jax.ShapeDtypeStruct(dims, dtype)


def place_stream(stream):
    return call(
        stream_kernel, shape(TOK, D), stream,
        scratch_shapes=[pltpu.VMEM((DZ, DZ), bf16)],
        cost_estimate=pl.CostEstimate(flops=2 * TOK * D * DZ, bytes_accessed=4 * TOK * D, transcendentals=0),
        limit=16 * 2**20,
    )


def place_hidden(hidden):
    return call(
        hidden_kernel, shape(NC, NZ, TOK, NXY * LANE), hidden,
        grid=(NZ,),
        in_specs=[pl.BlockSpec((TOK, FZ), lambda z: (0, z))],
        out_specs=pl.BlockSpec((NC, 1, TOK, NXY * LANE), lambda z: (0, z, 0, 0)),
        cost_estimate=pl.CostEstimate(flops=TOK * FF * 8, bytes_accessed=6 * TOK * FF, transcendentals=0),
        limit=60 * 2**20,
    )


def local(teacher, mine, other, hidden, stream):
    return call(
        main_kernel, (shape(NXY, NZ * BLK, LANE), shape(NXY, NZ * BLK, LANE)), teacher, mine, other, hidden, stream,
        in_specs=[SMEM, VMEM, VMEM, pl.BlockSpec(memory_space=pl.ANY), VMEM],
        scratch_shapes=[
            pltpu.VMEM((NC, NZ, TOK, NXY * LANE), bf16),
            pltpu.VMEM((R, D), bf16),
            pltpu.VMEM((8, D), f32),
            pltpu.VMEM((TOK, D), f32),
            pltpu.VMEM((8, D), f32),
            pltpu.VMEM((R, D), bf16),
            pltpu.VMEM((16, NCH * LANE), f32),
            pltpu.VMEM((TOK, D), bf16),
            pltpu.SemaphoreType.DMA((NC * NZ,)),
        ],
        limit=49 * 2**20,
    )


def body(hidden, stream, adapter_in, adapter_out, norm_gain, teacher):
    mine = call(
        pack_kernel, shape(NZ, BLK, LANE), adapter_in, adapter_out, norm_gain,
        scratch_shapes=[pltpu.VMEM((R, LANE), f32), pltpu.VMEM((LANE, LANE), f32)],
    )
    column = lax.all_to_all(mine, "zl", 0, 0, tiled=True)
    column = jnp.concatenate(
        [column[:, :R].reshape(1, TOP, LANE), column[:, R:].reshape(1, 8 * NZ, LANE)], axis=1
    )
    copies = jnp.broadcast_to(column, (NXY, NZ * BLK, LANE))
    mine = lax.all_to_all(copies, ("x", "y"), 0, 0, tiled=True)
    mine, hidden, stream = lax.optimization_barrier(
        (mine, place_hidden(hidden), place_stream(stream))
    )
    other = lax.ppermute(mine, "c", SWAP)
    keep, send = local(teacher, mine, other, hidden, stream)
    other = lax.ppermute(send, "c", SWAP)
    pairs = (keep.astype(f32) + other.astype(f32)).astype(bf16)
    parts = lax.all_to_all(pairs, ("x", "y"), 0, 0, tiled=True)
    part = jnp.sum(parts.astype(f32), axis=0).astype(bf16)
    part = jnp.concatenate(
        [part[:TOP].reshape(1, NZ, R, LANE), part[TOP:].reshape(1, NZ, 8, LANE)], axis=2
    )
    parts = jnp.broadcast_to(part, (NH, NZ, BLK, LANE)).reshape(NH * NZ, BLK, LANE)
    parts = lax.all_to_all(parts, ("zh", "zl"), 0, 0, tiled=True)
    shapes = (shape(R, WF, dtype=f32), shape(R, WD, dtype=f32), shape(1, WD, dtype=f32))
    return call(final_kernel, shapes, parts)


def solution(mesh):
    fine = Mesh(mesh.devices.reshape(NH, NZ, NX, NY, NC), ALL)
    return jax.shard_map(
        body,
        mesh=fine,
        in_specs=(P(ALL, None), P(ALL, None), P(None, DEV), P(None, DEV), P(None, DEV), P(ALL)),
        out_specs=(P(None, DEV), P(None, DEV), P(None, DEV)),
        check_vma=False,
    )
```
